32 devices in a mesh: dp: 8 (over z, x), tensor: 4 (over y, core).
Axes of the slice: x: 2, y: 2, z: 4, core: 2. Of those that a mesh axis runs over, the one named last changes fastest.
Arguments:
- hidden_in: bfloat16 [192, 4096], P('dp'), may hold values from -6 to 6
- queries: bfloat16 [192, 8192], P('dp', 'tensor'), may hold values from -150 to 150
- key_cache: bfloat16 [192, 4, 768, 128], P('dp', 'tensor'), may hold values from -5 to 5
- cached_value_rows: bfloat16 [192, 4, 768, 128], P('dp', 'tensor'), may hold values from -6 to 6
- cache_lengths: int32 [192], P('dp'), may hold values from 48 to 768, as said below
- out_weight: bfloat16 [8192, 4096], P('tensor', 'dp'), may hold values from -0.0625 to 0.0625
- expert_ids: int32 [192, 8], P('dp'), may hold values from 0 to 127, as said below
- route_probs: float32 [192, 8], P('dp'), may hold values from 0.05 to 1
- w_gate: bfloat16 [128, 4096, 768], P(('dp', 'tensor')), may hold values from -0.09375 to 0.09375
- w_up: bfloat16 [128, 4096, 768], P(('dp', 'tensor')), may hold values from -0.09375 to 0.09375
- w_down: bfloat16 [128, 768, 4096], P(('dp', 'tensor')), may hold values from -0.21875 to 0.21875
Outputs:
- layer_out: bfloat16 [192, 4096], P('dp', 'tensor')
The draws below stay inside these ranges and needn't reach their ends.
Inputs may be any that keep to these rules, and one draw needn't show every extreme that they name: `expert_ids`: each row names 8 different experts; among the rows of one index of dp no expert is named more than 2 times, and one expert is named exactly 2 times in every such group of rows. Row r attends to cache positions 0 to cache_lengths[r] - 1; some row has all 768.
All inputs are finite; a program needn't handle non-finite values.
Results may differ from the reference program's by a relative error of at most 0.01.
Values may be sent and summed in bfloat16 or wider, within the bound.
A program may use at most 128 MiB of HBM per device.

```python
import math
import jax
import jax.numpy as jnp
from jax import lax

D = 4096
QUERY_HEADS = 64
KEY_VALUE_HEADS = 4
HEAD_SIZE = 128
EXPERTS = 128
TOP = 8
FF = 768
CAP = 2
ROWS_DEV = 24
CACHE_POSITIONS = 768
BATCH_ROWS = 192
N_DP = 8


def draw_queries(key, part):
    value_rows = jnp.clip(jax.random.normal(jax.random.fold_in(key, 21), (BATCH_ROWS, QUERY_HEADS, HEAD_SIZE), jnp.float32), -4.0, 4.0)
    return value_rows.reshape(BATCH_ROWS, QUERY_HEADS * HEAD_SIZE).astype(jnp.bfloat16)


def draw_key_cache(key, part):
    value_rows = jnp.clip(jax.random.normal(jax.random.fold_in(key, 31), (BATCH_ROWS, KEY_VALUE_HEADS, CACHE_POSITIONS, HEAD_SIZE), jnp.float32), -4.0, 4.0)
    return value_rows.astype(jnp.bfloat16)


def draw_cache_lengths(key, part):
    blocks = BATCH_ROWS // ROWS_DEV
    full_block = jax.random.randint(jax.random.fold_in(key, 41), (), 0, blocks)
    caps = jax.random.randint(jax.random.fold_in(key, 42), (blocks,), CACHE_POSITIONS // 4, CACHE_POSITIONS + 1)
    caps = jnp.where(jnp.arange(blocks, dtype=jnp.int32) == full_block, CACHE_POSITIONS, caps)
    row_caps = jnp.repeat(caps, ROWS_DEV)
    lengths = jax.random.randint(jax.random.fold_in(key, 43), (BATCH_ROWS,), CACHE_POSITIONS // 16, row_caps + 1)
    longest = jnp.repeat(jax.random.randint(jax.random.fold_in(key, 44), (blocks,), 0, ROWS_DEV), ROWS_DEV)
    within = jnp.arange(BATCH_ROWS, dtype=jnp.int32) % ROWS_DEV
    return jnp.where(within == longest, row_caps, lengths).astype(jnp.int32)


def draw_expert_ids(key, part):
    blocks = BATCH_ROWS // ROWS_DEV
    total = ROWS_DEV * TOP
    hottest = jax.random.randint(jax.random.fold_in(key, 51), (), 0, EXPERTS)

    def one_block(block_key):
        order = jax.random.permutation(jax.random.fold_in(block_key, 1), EXPERTS).astype(jnp.int32)
        order = jnp.where(order == hottest, order[0], order)
        order = order.at[0].set(hottest)
        doubled = jax.random.randint(jax.random.fold_in(block_key, 2), (), max(1, total - EXPERTS), total // 2 + 1)
        position = jnp.arange(EXPERTS, dtype=jnp.int32)
        counts = jnp.where(position < doubled, 2, jnp.where(position < total - doubled, 1, 0)).astype(jnp.int32)
        ends = jnp.cumsum(counts)
        entry = jnp.searchsorted(ends, jnp.arange(total, dtype=jnp.int32), side='right')
        multiset = order[entry]
        table = multiset.reshape(TOP, ROWS_DEV).T
        shuffle = jax.random.permutation(jax.random.fold_in(block_key, 3), ROWS_DEV)
        return table[shuffle]
    block_keys = jax.random.split(jax.random.fold_in(key, 52), blocks)
    return jax.vmap(one_block)(block_keys).reshape(BATCH_ROWS, TOP).astype(jnp.int32)


def block_levels(own_key, shape, cuts, low, high):
    def one(axis_at, shards_of):
        draws = jax.random.uniform(jax.random.fold_in(jax.random.fold_in(own_key, 6), axis_at), (shards_of,), jnp.float32, low / len(cuts), high / len(cuts))
        return jnp.repeat(jnp.exp(draws), shape[axis_at] // shards_of).reshape((-1,) + (1,) * (len(shape) - axis_at - 1))

    loudness = one(*cuts[0])
    for cut in cuts[1:]:
        loudness = loudness * one(*cut)
    return loudness


def noise(key, shape, scale, most, pieces=(), kind=jnp.bfloat16):
    entries = jax.random.normal(key, shape, jnp.float32) * scale
    if len(pieces) > 0:
        entries = block_levels(key, shape, pieces, -0.22, 0.18) * entries
    return jnp.clip(entries, min=-most, max=most).astype(kind)


def setup_inputs(seed: int = 0) -> dict:
    key_of = jax.random.split(jax.random.key(seed), 12)
    hidden_in = noise(key_of[0], (BATCH_ROWS, D), 1.0, 6.0, ((0, 8),))
    queries = draw_queries(jax.random.fold_in(key_of[11], 71), 0)
    key_cache = draw_key_cache(jax.random.fold_in(key_of[11], 71), 0)
    cached_value_rows = noise(key_of[3], (BATCH_ROWS, KEY_VALUE_HEADS, CACHE_POSITIONS, HEAD_SIZE), 1.0, 6.0, ((0, 8), (1, 4)))
    cache_lengths = draw_cache_lengths(jax.random.fold_in(key_of[11], 71), 0)
    out_weight = noise(key_of[5], (QUERY_HEADS * HEAD_SIZE, D), (QUERY_HEADS * HEAD_SIZE) ** -0.5, 0.0625, ((0, 4), (1, 8)))
    expert_ids = draw_expert_ids(jax.random.fold_in(key_of[11], 71), 0)
    route_probs = jnp.clip(jnp.exp(math.log(1.0) - 2.9957323 * jax.random.uniform(key_of[7], (BATCH_ROWS, TOP), jnp.float32) ** block_levels(key_of[7], (BATCH_ROWS, TOP), ((0, 8),), -0.2, 0.2)), 0.05, 1.0)
    w_gate = noise(key_of[8], (EXPERTS, D, FF), D ** -0.5, 0.09375, ((0, 32),))
    w_up = noise(key_of[9], (EXPERTS, D, FF), D ** -0.5, 0.09375, ((0, 32),))
    w_down = noise(key_of[10], (EXPERTS, FF, D), FF ** -0.5, 0.21875, ((0, 32),))
    return {"hidden_in": hidden_in, "queries": queries, "key_cache": key_cache, "cached_value_rows": cached_value_rows, "cache_lengths": cache_lengths, "out_weight": out_weight, "expert_ids": expert_ids, "route_probs": route_probs, "w_gate": w_gate, "w_up": w_up, "w_down": w_down}


def reference(hidden_in, queries, key_cache, cached_value_rows, cache_lengths, out_weight, expert_ids, route_probs, w_gate, w_up, w_down):
    group_width = QUERY_HEADS // KEY_VALUE_HEADS
    score_scale = 1.0 / math.sqrt(HEAD_SIZE)
    query_head_count = queries.astype(jnp.float32).reshape(BATCH_ROWS, KEY_VALUE_HEADS, group_width, HEAD_SIZE).transpose(1, 0, 2, 3)
    valid_mask = (jnp.arange(CACHE_POSITIONS, dtype=jnp.int32)[None, :] < cache_lengths.astype(jnp.int32)[:, None])[:, None, :]

    def attend(operands):
        query_one, keys_one, values_one = operands
        scores = jnp.einsum('rgd,rld->rgl', query_one, keys_one.astype(jnp.float32)) * score_scale
        scores = jnp.where(valid_mask, scores, -jnp.inf)
        largest = lax.optimization_barrier(jnp.max(scores, axis=-1, keepdims=True))
        exponent = jnp.exp(scores - largest)
        attn_probs = (exponent / lax.optimization_barrier(jnp.sum(exponent, axis=-1, keepdims=True))).astype(jnp.bfloat16)
        return jnp.einsum('rgl,rld->rgd', attn_probs.astype(jnp.float32), values_one.astype(jnp.float32)).astype(jnp.bfloat16)
    heads_out = lax.map(attend, (query_head_count, key_cache.transpose(1, 0, 2, 3), cached_value_rows.transpose(1, 0, 2, 3)))
    attn_out = heads_out.transpose(1, 0, 2, 3).reshape(BATCH_ROWS, QUERY_HEADS * HEAD_SIZE)
    projected = jnp.dot(attn_out, out_weight, preferred_element_type=jnp.float32).astype(jnp.bfloat16)
    residual = (hidden_in.astype(jnp.float32) + projected.astype(jnp.float32)).astype(jnp.bfloat16)
    resid_f = residual.astype(jnp.float32)
    normed = (resid_f * lax.rsqrt(lax.optimization_barrier(jnp.mean(resid_f * resid_f, axis=-1, keepdims=True)) + 1e-06)).astype(jnp.bfloat16)
    route_weights = route_probs / lax.optimization_barrier(jnp.sum(route_probs, axis=-1, keepdims=True))
    slots_all = N_DP * CAP

    def one_expert(mixture, operands):
        gate_one, up_one, down_one, expert = operands
        member = expert_ids == expert
        weight_row = lax.optimization_barrier(jnp.sum(jnp.where(member, route_weights, 0.0), axis=-1))
        chosen = jnp.any(member, axis=-1)
        row_index = jnp.nonzero(chosen, size=slots_all, fill_value=0)[0].astype(jnp.int32)
        live_slot = jnp.arange(slots_all, dtype=jnp.int32) < jnp.sum(chosen.astype(jnp.int32))
        rows_in = normed[row_index]
        gate_proj = jnp.dot(rows_in, gate_one, preferred_element_type=jnp.float32)
        up_proj = jnp.dot(rows_in, up_one, preferred_element_type=jnp.float32)
        activated = (jax.nn.silu(gate_proj) * up_proj).astype(jnp.bfloat16)
        expert_out = jnp.dot(activated, down_one, preferred_element_type=jnp.float32).astype(jnp.bfloat16)
        scaled = jnp.where(live_slot, weight_row[row_index], 0.0)[:, None] * expert_out.astype(jnp.float32)
        return (mixture.at[row_index].add(scaled), None)
    mixture, unused = lax.scan(one_expert, jnp.zeros((BATCH_ROWS, D), jnp.float32), (w_gate, w_up, w_down, jnp.arange(EXPERTS, dtype=jnp.int32)))
    return (resid_f + mixture).astype(jnp.bfloat16)
```

```python
import functools
import math

import jax
import jax.numpy as jnp
from jax import lax
from jax.experimental import pallas as pl
from jax.experimental.pallas import tpu as pltpu
from jax.sharding import PartitionSpec as P

CAP = 2
SUB = 512
MESH = pl.DeviceIdType.MESH


def layer_kernel(
    G,
    T,
    E,
    R,
    attn_ref,
    hidden_ref,
    pick_ref,
    table_ref,
    wo_hbm,
    wg_hbm,
    wu_hbm,
    wd_hbm,
    out_ref,
    wo,
    wg,
    wu,
    wd,
    gathered,
    partial,
    rs_recv,
    summed,
    proj,
    residual,
    normed,
    outgoing,
    arrived,
    acc_g,
    acc_u,
    act,
    outs,
    results,
    wo_sem,
    wg_sem,
    wu_sem,
    wd_sem,
    s1,
    r1,
    s2,
    r2,
    s3,
    r3,
    s4,
    r4,
    s5,
    r5,
):
    d = lax.axis_index("dp")
    t = lax.axis_index("tensor")
    rows, width = hidden_ref.shape
    share = width // T
    cb = wo.shape[1]
    per = G // T
    ff = wg.shape[2]
    subs = share // SUB
    f32 = jnp.float32
    bf16 = jnp.bfloat16

    def remote(src, dst, ss, rs, dd, tt):
        return pltpu.make_async_remote_copy(
            src_ref=src,
            dst_ref=dst,
            send_sem=ss,
            recv_sem=rs,
            device_id=(dd, tt),
            device_id_type=MESH,
        )

    barrier = pltpu.get_barrier_semaphore()

    def greet(i, c):
        o = lax.rem(d * T + t + i, G * T)
        pl.semaphore_signal(barrier, inc=1, device_id=(o // T, lax.rem(o, T)), device_id_type=MESH)
        return c

    lax.fori_loop(1, G * T, greet, 0)

    wo_copy = pltpu.make_async_copy(wo_hbm, wo, wo_sem)
    wo_copy.start()

    def part(j):
        return pl.ds(j * share, share)

    def g_copy(j):
        return pltpu.make_async_copy(wg_hbm.at[:, part(j), :], wg.at[:, part(j), :], wg_sem.at[j])

    def u_copy(j):
        return pltpu.make_async_copy(wu_hbm.at[:, part(j), :], wu.at[:, part(j), :], wu_sem.at[j])

    def d_copy(s):
        j = lax.rem(t + 1 + s // subs, T)
        col = pl.multiple_of(j * share + (s % subs) * SUB, SUB)
        return pltpu.make_async_copy(
            wd_hbm.at[:, :, pl.ds(col, SUB)], wd.at[s % 2], wd_sem.at[s % 2]
        )

    pl.semaphore_wait(barrier, G * T - 1)

    def send1(i, c):
        p = lax.rem(d + i, G)
        remote(attn_ref, gathered.at[d], s1.at[p], r1.at[d], p, t).start()
        return c

    lax.fori_loop(1, G, send1, 0)
    for j in range(T):
        g_copy(j).start()
        u_copy(j).start()
    d_copy(0).start()
    d_copy(1).start()
    gathered[d] = attn_ref[...]
    wo_copy.wait()

    def project(i, c):
        g = lax.rem(d + G - i, G)

        @pl.when(i > 0)
        def _():
            remote(attn_ref, gathered.at[g], s1.at[g], r1.at[g], g, t).wait_recv()

        partial[g] = jnp.dot(gathered[g], wo[...], preferred_element_type=f32).astype(bf16)
        owner = g // per

        @pl.when(owner != t)
        def _():
            remote(
                partial.at[g], rs_recv.at[t, lax.rem(g, per)], s2.at[g], r2.at[t, lax.rem(g, per)], d, owner
            ).start()

        return c

    lax.fori_loop(0, G, project, 0)

    def reduce(k, c):
        g = t * per + k
        total = partial[g].astype(f32)
        for o in range(1, T):
            src = lax.rem(t + o, T)
            remote(partial.at[g], rs_recv.at[src, k], s2.at[g], r2.at[src, k], d, src).wait_recv()
            total = total + rs_recv[src, k].astype(f32)
        summed[k] = total.astype(bf16)
        for tt in range(T):
            own = jnp.logical_and(g == d, t == tt)

            @pl.when(own)
            def _():
                proj[d] = summed[k]

            @pl.when(jnp.logical_not(own))
            def _():
                remote(summed.at[k], proj.at[d], s3.at[k, tt], r3.at[d], g, tt).start()

        return c

    lax.fori_loop(0, per, reduce, 0)

    home = d // per

    def wait3(i, c):
        @pl.when(jnp.logical_not(jnp.logical_and(i == d, home == t)))
        def _():
            remote(summed.at[0], proj.at[i], s3.at[0, 0], r3.at[i], i, home).wait_recv()

        return c

    lax.fori_loop(0, G, wait3, 0)

    squares = jnp.zeros((rows, cb), f32)
    for g in range(G):
        cols = slice(g * cb, (g + 1) * cb)
        block = (hidden_ref[:, cols].astype(f32) + proj[g].astype(f32)).astype(bf16)
        residual[:, cols] = block
        bf = block.astype(f32)
        squares = squares + bf * bf
    scale = lax.rsqrt(jnp.sum(squares, axis=-1, keepdims=True) / width + 1e-06)
    for g in range(G):
        cols = slice(g * cb, (g + 1) * cb)
        normed[:, cols] = (residual[:, cols].astype(f32) * scale).astype(bf16)

    for j in range(T):
        block = jnp.dot(
            pick_ref[...], normed[:, j * share : (j + 1) * share], preferred_element_type=f32
        )
        outgoing[j] = block.reshape(G, R, share).astype(bf16)
        arrived[j, d] = outgoing[j, d]

        def send4(i, c, j=j):
            p = lax.rem(d + i, G)
            remote(outgoing.at[j, p], arrived.at[j, d], s4.at[j, p], r4.at[j, d], p, t).start()
            return c

        lax.fori_loop(1, G, send4, 0)

    for j in range(T):

        def wait4(i, c, j=j):
            p = lax.rem(d + G - i, G)
            remote(outgoing.at[j, p], arrived.at[j, p], s4.at[j, p], r4.at[j, p], p, t).wait_recv()
            return c

        lax.fori_loop(1, G, wait4, 0)
        g_copy(j).wait()
        u_copy(j).wait()

        def up(e, c, j=j):
            x = arrived[j].astype(f32).reshape(G * R, share).astype(bf16)
            gp = jnp.dot(x, wg[e, j * share : (j + 1) * share, :], preferred_element_type=f32)
            uq = jnp.dot(x, wu[e, j * share : (j + 1) * share, :], preferred_element_type=f32)
            if j == 0:
                acc_g[e] = gp
                acc_u[e] = uq
            else:
                gp = acc_g[e] + gp
                uq = acc_u[e] + uq
                if j < T - 1:
                    acc_g[e] = gp
                    acc_u[e] = uq
                else:
                    slot = lax.rem(lax.broadcasted_iota(jnp.int32, (G * R, ff), 0), R)
                    mine = (slot // CAP) == e
                    value = gp / (1.0 + jnp.exp(-gp)) * uq
                    act[e] = jnp.where(mine, value, 0.0).astype(bf16)
            return c

        lax.fori_loop(0, E, up, 0)

    for s in range(T * subs):
        d_copy(s).wait()
        half = s % subs
        total = jnp.dot(act[0], wd[s % 2, 0], preferred_element_type=f32)
        for e in range(1, E):
            total = total + jnp.dot(act[e], wd[s % 2, e], preferred_element_type=f32)
        n = s // subs
        outs[n, :, :, half * SUB : (half + 1) * SUB] = total.reshape(G, R, SUB).astype(bf16)
        if s + 2 < T * subs:
            d_copy(s + 2).start()
        if half == subs - 1:
            j = lax.rem(t + 1 + n, T)

            def send5(i, c, n=n, j=j):
                p = lax.rem(d + i, G)
                own = jnp.logical_and(p == d, j == t)

                @pl.when(own)
                def _():
                    results[d, t] = outs[n, p]

                @pl.when(jnp.logical_not(own))
                def _():
                    remote(
                        outs.at[n, p], results.at[d, t], s5.at[n, p], r5.at[d, t], p, j
                    ).start()

                return c

            lax.fori_loop(0, G, send5, 0)

    def wait5(i, c):
        o = lax.rem(d * T + t + i, G * T)
        p, q = o // T, lax.rem(o, T)
        remote(outs.at[0, p], results.at[p, q], s5.at[0, p], r5.at[p, q], p, q).wait_recv()
        return c

    lax.fori_loop(1, G * T, wait5, 0)
    back = results[...].astype(f32).reshape(G * T * R, share)
    mixture = jnp.dot(
        table_ref[...], back, precision=lax.Precision.HIGHEST, preferred_element_type=f32
    )
    mine = residual[:, pl.ds(pl.multiple_of(t * share, share), share)].astype(f32)
    out_ref[...] = (mine + mixture).astype(bf16)

    def drain1(i, c):
        p = lax.rem(d + i, G)
        remote(attn_ref, gathered.at[d], s1.at[p], r1.at[d], p, t).wait_send()
        for j in range(T):
            remote(outgoing.at[j, p], arrived.at[j, d], s4.at[j, p], r4.at[j, d], p, t).wait_send()
        return c

    lax.fori_loop(1, G, drain1, 0)

    def drain2(g, c):
        owner = g // per

        @pl.when(owner != t)
        def _():
            remote(partial.at[g], rs_recv.at[t, 0], s2.at[g], r2.at[t, 0], d, owner).wait_send()

        for n in range(T):
            j = lax.rem(t + 1 + n, T)

            @pl.when(jnp.logical_not(jnp.logical_and(g == d, j == t)))
            def _():
                remote(outs.at[n, g], results.at[d, t], s5.at[n, g], r5.at[d, t], g, j).wait_send()

        return c

    lax.fori_loop(0, G, drain2, 0)

    def drain3(k, c):
        g = t * per + k
        for tt in range(T):

            @pl.when(jnp.logical_not(jnp.logical_and(g == d, t == tt)))
            def _():
                remote(summed.at[k], proj.at[d], s3.at[k, tt], r3.at[d], g, tt).wait_send()

        return c

    lax.fori_loop(0, per, drain3, 0)


def local(
    hidden_in,
    queries,
    key_cache,
    cached_value_rows,
    cache_lengths,
    out_weight,
    expert_ids,
    route_probs,
    w_gate,
    w_up,
    w_down,
):
    G = lax.axis_size("dp")
    T = lax.axis_size("tensor")
    tp_rank = lax.axis_index("tensor")
    rows_dev, kv_local, cache_len, head_dim = key_cache.shape
    groups = queries.shape[1] // (kv_local * head_dim)
    width = hidden_in.shape[1]
    query_heads = queries.reshape(rows_dev, kv_local, groups, head_dim)
    scores = jnp.einsum(
        "rhgd,rhld->rhgl", query_heads, key_cache, preferred_element_type=jnp.float32
    ) * (1.0 / math.sqrt(head_dim))
    valid_mask = (jnp.arange(cache_len, dtype=jnp.int32)[None, :] < cache_lengths[:, None])[
        :, None, None, :
    ]
    scores = jnp.where(valid_mask, scores, -jnp.inf)
    largest = jnp.max(scores, axis=-1, keepdims=True)
    exponent = jnp.exp(scores - largest)
    attn_probs = (exponent / jnp.sum(exponent, axis=-1, keepdims=True)).astype(jnp.bfloat16)
    attn_out = jnp.einsum(
        "rhgl,rhld->rhgd", attn_probs, cached_value_rows, preferred_element_type=jnp.float32
    ).astype(jnp.bfloat16)
    attn_out = attn_out.reshape(rows_dev, kv_local * groups * head_dim)

    E, _, ff = w_gate.shape
    experts = G * T * E
    R = max(8, E * CAP)
    matches = expert_ids[:, :, None] == jnp.arange(experts, dtype=jnp.int32)[None, None, :]
    assigned = jnp.sum(matches.astype(jnp.int32), axis=1)
    slot_rank = jnp.cumsum(assigned, axis=0) - assigned
    slot_hit = (slot_rank[:, :, None] == jnp.arange(CAP, dtype=jnp.int32)[None, None, :]) & (
        assigned[:, :, None] > 0
    )
    route_weights = route_probs / jnp.sum(route_probs, axis=-1, keepdims=True)
    weight = jnp.sum(jnp.where(matches, route_weights[:, :, None], 0.0), axis=1)
    table = jnp.where(slot_hit, weight[:, :, None], 0.0).reshape(rows_dev, G * T, E * CAP)
    table = jnp.pad(table, ((0, 0), (0, 0), (0, R - E * CAP))).reshape(rows_dev, G * T * R)
    hit = slot_hit.astype(jnp.bfloat16).reshape(rows_dev, G, T, E * CAP)
    pick = lax.dynamic_index_in_dim(hit, tp_rank, 2, keepdims=False)
    pick = jnp.pad(pick, ((0, 0), (0, 0), (0, R - E * CAP))).reshape(rows_dev, G * R).T

    share = width // T
    hl = attn_out.shape[1]
    cb = out_weight.shape[1]
    per = G // T
    bf16 = jnp.bfloat16
    f32 = jnp.float32
    vmem = pl.BlockSpec(memory_space=pltpu.VMEM)
    hbm = pl.BlockSpec(memory_space=pl.ANY)
    dma = pltpu.SemaphoreType.DMA
    return pl.pallas_call(
        functools.partial(layer_kernel, G, T, E, R),
        out_shape=jax.ShapeDtypeStruct((rows_dev, share), bf16),
        in_specs=[vmem] * 4 + [hbm] * 4,
        out_specs=vmem,
        scratch_shapes=[
            pltpu.VMEM((hl, cb), bf16),
            pltpu.VMEM((E, width, ff), bf16),
            pltpu.VMEM((E, width, ff), bf16),
            pltpu.VMEM((2, E, ff, SUB), bf16),
            pltpu.VMEM((G, rows_dev, hl), bf16),
            pltpu.VMEM((G, rows_dev, cb), bf16),
            pltpu.VMEM((T, per, rows_dev, cb), bf16),
            pltpu.VMEM((per, rows_dev, cb), bf16),
            pltpu.VMEM((G, rows_dev, cb), bf16),
            pltpu.VMEM((rows_dev, width), bf16),
            pltpu.VMEM((rows_dev, width), bf16),
            pltpu.VMEM((T, G, R, share), bf16),
            pltpu.VMEM((T, G, R, share), bf16),
            pltpu.VMEM((E, G * R, ff), f32),
            pltpu.VMEM((E, G * R, ff), f32),
            pltpu.VMEM((E, G * R, ff), bf16),
            pltpu.VMEM((T, G, R, share), bf16),
            pltpu.VMEM((G, T, R, share), bf16),
            dma(()),
            dma((T,)),
            dma((T,)),
            dma((2,)),
            dma((G,)),
            dma((G,)),
            dma((G,)),
            dma((T, per)),
            dma((per, T)),
            dma((G,)),
            dma((T, G)),
            dma((T, G)),
            dma((T, G)),
            dma((G, T)),
        ],
        compiler_params=pltpu.CompilerParams(
            collective_id=0, has_side_effects=True, vmem_limit_bytes=66 * 1000 * 1000
        ),
    )(attn_out, hidden_in, pick, table, out_weight, w_gate, w_up, w_down)


def solution(mesh):
    placed = (
        P("dp", None),
        P("dp", "tensor"),
        P("dp", "tensor", None, None),
        P("dp", "tensor", None, None),
        P("dp"),
        P("tensor", "dp"),
        P("dp", None),
        P("dp", None),
        P(("dp", "tensor"), None, None),
        P(("dp", "tensor"), None, None),
        P(("dp", "tensor"), None, None),
    )
    return jax.shard_map(
        local, mesh=mesh, in_specs=placed, out_specs=P("dp", "tensor"), check_vma=False
    )
```

```python
import functools
import math

import jax
import jax.numpy as jnp
from jax import lax
from jax.experimental import pallas as pl
from jax.experimental.pallas import tpu as pltpu
from jax.sharding import PartitionSpec as P

CAP = 2
SUB = 512
INNER = 2
MESH = pl.DeviceIdType.MESH


def layer_kernel(
    G,
    T,
    E,
    R,
    attn_ref,
    hidden_ref,
    ids_ref,
    probs_ref,
    wo_hbm,
    wg_hbm,
    wu_hbm,
    wd_hbm,
    out_ref,
    wo,
    wg,
    wu,
    wd,
    gathered,
    partial,
    rs_recv,
    summed,
    proj,
    residual,
    normed,
    outgoing,
    arrived,
    acc_g,
    acc_u,
    act,
    outs,
    results,
    pick,
    table,
    wo_sem,
    wg_sem,
    wu_sem,
    wd_sem,
    s1,
    r1,
    sf,
    s2,
    r2,
    s3,
    r3,
    s4,
    r4,
    s5,
    r5,
):
    d = lax.axis_index("dp")
    t = lax.axis_index("tensor")
    rows, width = hidden_ref.shape
    share = width // T
    cb = wo.shape[1]
    per = G // T
    ff = wg.shape[2]
    subs = share // SUB
    f32 = jnp.float32
    bf16 = jnp.bfloat16

    def remote(src, dst, ss, rs, dd, tt):
        return pltpu.make_async_remote_copy(
            src_ref=src,
            dst_ref=dst,
            send_sem=ss,
            recv_sem=rs,
            device_id=(dd, tt),
            device_id_type=MESH,
        )

    barrier = pltpu.get_barrier_semaphore()

    def greet(i, c):
        o = lax.rem(d * T + t + i, G * T)
        pl.semaphore_signal(barrier, inc=1, device_id=(o // T, lax.rem(o, T)), device_id_type=MESH)
        return c

    lax.fori_loop(1, G * T, greet, 0)

    wo_copy = pltpu.make_async_copy(wo_hbm, wo, wo_sem)
    wo_copy.start()

    def part(j):
        return pl.ds(j * share, share)

    def g_copy(j):
        return pltpu.make_async_copy(wg_hbm.at[:, part(j), :], wg.at[:, part(j), :], wg_sem.at[j])

    def u_copy(j):
        return pltpu.make_async_copy(wu_hbm.at[:, part(j), :], wu.at[:, part(j), :], wu_sem.at[j])

    def d_copy(s):
        j = lax.rem(t + 1 + s // subs, T)
        col = pl.multiple_of(j * share + (s % subs) * SUB, SUB)
        return pltpu.make_async_copy(wd_hbm.at[:, :, pl.ds(col, SUB)], down_at(s), wd_sem.at[s])

    def down_at(s):
        if s < 2:
            return wd.at[s]
        k = (s - 2) // 2
        return (wg, wu)[s % 2].at[:, k * share : k * share + ff, 0:SUB]

    subs_all = T * subs

    pl.semaphore_wait(barrier, G * T - 1)

    outer = G // INNER
    inner = lax.rem(d, INNER)
    mate = d + 1 - 2 * inner

    def far(i):
        return lax.rem(d + INNER * i, G)

    def first(p):
        return remote(attn_ref, gathered.at[d], s1.at[p], r1.at[d], p, t)

    first(mate).start()

    def send1(i, c):
        first(far(i)).start()
        return c

    lax.fori_loop(1, outer, send1, 0)
    for j in range(T):
        g_copy(j).start()
        u_copy(j).start()
    d_copy(0).start()
    d_copy(1).start()
    gathered[d] = attn_ref[...]

    ids = ids_ref[...]
    probs = probs_ref[...]
    shares = probs / jnp.sum(probs, axis=-1, keepdims=True)
    below = lax.broadcasted_iota(jnp.int32, (rows, rows), 0) > lax.broadcasted_iota(
        jnp.int32, (rows, rows), 1
    )
    below = jnp.where(below, 1.0, 0.0).astype(bf16)

    def routes(count, device_of):
        col = lax.broadcasted_iota(jnp.int32, (rows, count), 1)
        place = lax.rem(col, R)
        expert = device_of(lax.div(col, R)) * E + lax.div(place, CAP)
        slot = lax.rem(place, CAP)
        assigned = jnp.zeros((rows, count), f32)
        weight = jnp.zeros((rows, count), f32)
        for k in range(ids.shape[1]):
            same = ids[:, k : k + 1] == expert
            assigned = assigned + jnp.where(same, 1.0, 0.0)
            weight = weight + jnp.where(same, shares[:, k : k + 1], 0.0)
        rank = jnp.dot(below, assigned.astype(bf16), preferred_element_type=f32)
        hit = (assigned > 0.5) & (rank.astype(jnp.int32) == slot) & (place < E * CAP)
        return hit, weight

    hit, weight = routes(G * T * R, lambda n: n)
    table[...] = jnp.where(hit, weight, 0.0)
    hit, weight = routes(G * R, lambda n: n * T + t)
    pick[...] = jnp.where(hit, 1.0, 0.0).astype(bf16)
    wo_copy.wait()

    def project(i, c):
        near = i < outer + 1
        k = jnp.where(near, i - 1, i - outer)
        base = lax.rem(d + G - INNER * k, G)
        straight = jnp.logical_and(i > 1, near)
        g = jnp.where(i == 0, d, jnp.where(straight, base, base + 1 - 2 * inner))

        @pl.when(i > 0)
        def _():
            remote(attn_ref, gathered.at[g], s1.at[g], r1.at[g], g, t).wait_recv()

        @pl.when(straight)
        def _():
            remote(gathered.at[g], gathered.at[g], sf.at[g], r1.at[g], mate, t).start()

        partial[g] = jnp.dot(gathered[g], wo[...], preferred_element_type=f32).astype(bf16)
        owner = g // per

        @pl.when(owner != t)
        def _():
            remote(
                partial.at[g], rs_recv.at[t, lax.rem(g, per)], s2.at[g], r2.at[t, lax.rem(g, per)], d, owner
            ).start()

        return c

    lax.fori_loop(0, G, project, 0)

    def reduce(k, c):
        g = t * per + k
        total = partial[g].astype(f32)
        for o in range(1, T):
            src = lax.rem(t + o, T)
            remote(partial.at[g], rs_recv.at[src, k], s2.at[g], r2.at[src, k], d, src).wait_recv()
            total = total + rs_recv[src, k].astype(f32)
        summed[k] = total.astype(bf16)
        for tt in range(T):
            own = jnp.logical_and(g == d, t == tt)

            @pl.when(own)
            def _():
                proj[d] = summed[k]

            @pl.when(jnp.logical_not(own))
            def _():
                remote(summed.at[k], proj.at[d], s3.at[k, tt], r3.at[d], g, tt).start()

        return c

    lax.fori_loop(0, per, reduce, 0)

    home = d // per

    def wait3(i, c):
        @pl.when(jnp.logical_not(jnp.logical_and(i == d, home == t)))
        def _():
            remote(summed.at[0], proj.at[i], s3.at[0, 0], r3.at[i], i, home).wait_recv()

        return c

    lax.fori_loop(0, G, wait3, 0)

    squares = jnp.zeros((rows, cb), f32)
    for g in range(G):
        cols = slice(g * cb, (g + 1) * cb)
        block = (hidden_ref[:, cols].astype(f32) + proj[g].astype(f32)).astype(bf16)
        residual[:, cols] = block
        bf = block.astype(f32)
        squares = squares + bf * bf
    scale = lax.rsqrt(jnp.sum(squares, axis=-1, keepdims=True) / width + 1e-06)
    for g in range(G):
        cols = slice(g * cb, (g + 1) * cb)
        normed[:, cols] = (residual[:, cols].astype(f32) * scale).astype(bf16)

    for j in range(T):
        block = lax.dot_general(
            pick[...],
            normed[:, j * share : (j + 1) * share],
            (((0,), (0,)), ((), ())),
            preferred_element_type=f32,
        )
        outgoing[j] = block.reshape(G, R, share).astype(bf16)
        arrived[j, d] = outgoing[j, d]

        def send4(i, c, j=j):
            p = lax.rem(d + i, G)
            remote(outgoing.at[j, p], arrived.at[j, d], s4.at[j, p], r4.at[j, d], p, t).start()
            return c

        lax.fori_loop(1, G, send4, 0)

    for j in range(T):

        def wait4(i, c, j=j):
            p = lax.rem(d + G - i, G)
            remote(outgoing.at[j, p], arrived.at[j, p], s4.at[j, p], r4.at[j, p], p, t).wait_recv()
            return c

        lax.fori_loop(1, G, wait4, 0)
        g_copy(j).wait()
        u_copy(j).wait()

        def up(e, c, j=j):
            x = arrived[j].astype(f32).reshape(G * R, share).astype(bf16)
            gp = jnp.dot(x, wg[e, j * share : (j + 1) * share, :], preferred_element_type=f32)
            uq = jnp.dot(x, wu[e, j * share : (j + 1) * share, :], preferred_element_type=f32)
            if j == 0:
                acc_g[e] = gp
                acc_u[e] = uq
            else:
                gp = acc_g[e] + gp
                uq = acc_u[e] + uq
                if j < T - 1:
                    acc_g[e] = gp
                    acc_u[e] = uq
                else:
                    slot = lax.rem(lax.broadcasted_iota(jnp.int32, (G * R, ff), 0), R)
                    mine = (slot // CAP) == e
                    value = gp / (1.0 + jnp.exp(-gp)) * uq
                    act[e] = jnp.where(mine, value, 0.0).astype(bf16)
            return c

        lax.fori_loop(0, E, up, 0)
        for s in (2 * j + 2, 2 * j + 3):
            if s < subs_all:
                d_copy(s).start()

    for s in range(T * subs):
        d_copy(s).wait()
        half = s % subs
        down = down_at(s)
        total = jnp.dot(act[0], down[0], preferred_element_type=f32)
        for e in range(1, E):
            total = total + jnp.dot(act[e], down[e], preferred_element_type=f32)
        n = s // subs
        outs[n, :, :, half * SUB : (half + 1) * SUB] = total.reshape(G, R, SUB).astype(bf16)
        if half == subs - 1:
            j = lax.rem(t + 1 + n, T)

            def send5(i, c, n=n, j=j):
                p = lax.rem(d + i, G)
                own = jnp.logical_and(p == d, j == t)

                @pl.when(own)
                def _():
                    results[d, t] = outs[n, p]

                @pl.when(jnp.logical_not(own))
                def _():
                    remote(
                        outs.at[n, p], results.at[d, t], s5.at[n, p], r5.at[d, t], p, j
                    ).start()

                return c

            lax.fori_loop(0, G, send5, 0)

    def wait5(i, c):
        o = lax.rem(d * T + t + i, G * T)
        p, q = o // T, lax.rem(o, T)
        remote(outs.at[0, p], results.at[p, q], s5.at[0, p], r5.at[p, q], p, q).wait_recv()
        return c

    lax.fori_loop(1, G * T, wait5, 0)
    back = results[...].astype(f32).reshape(G * T * R, share)
    mixture = jnp.dot(
        table[...], back, precision=lax.Precision.HIGHEST, preferred_element_type=f32
    )
    mine = residual[:, pl.ds(pl.multiple_of(t * share, share), share)].astype(f32)
    out_ref[...] = (mine + mixture).astype(bf16)

    def drain1(i, c):
        p = lax.rem(d + i, G)
        for j in range(T):
            remote(outgoing.at[j, p], arrived.at[j, d], s4.at[j, p], r4.at[j, d], p, t).wait_send()
        return c

    lax.fori_loop(1, G, drain1, 0)
    first(mate).wait_send()

    def drain0(i, c):
        first(far(i)).wait_send()
        g = far(i)
        remote(gathered.at[g], gathered.at[g], sf.at[g], r1.at[g], mate, t).wait_send()
        return c

    lax.fori_loop(1, outer, drain0, 0)

    def drain2(g, c):
        owner = g // per

        @pl.when(owner != t)
        def _():
            remote(partial.at[g], rs_recv.at[t, 0], s2.at[g], r2.at[t, 0], d, owner).wait_send()

        for n in range(T):
            j = lax.rem(t + 1 + n, T)

            @pl.when(jnp.logical_not(jnp.logical_and(g == d, j == t)))
            def _():
                remote(outs.at[n, g], results.at[d, t], s5.at[n, g], r5.at[d, t], g, j).wait_send()

        return c

    lax.fori_loop(0, G, drain2, 0)

    def drain3(k, c):
        g = t * per + k
        for tt in range(T):

            @pl.when(jnp.logical_not(jnp.logical_and(g == d, t == tt)))
            def _():
                remote(summed.at[k], proj.at[d], s3.at[k, tt], r3.at[d], g, tt).wait_send()

        return c

    lax.fori_loop(0, per, drain3, 0)


def local(
    hidden_in,
    queries,
    key_cache,
    cached_value_rows,
    cache_lengths,
    out_weight,
    expert_ids,
    route_probs,
    w_gate,
    w_up,
    w_down,
):
    G = lax.axis_size("dp")
    T = lax.axis_size("tensor")
    tp_rank = lax.axis_index("tensor")
    rows_dev, kv_local, cache_len, head_dim = key_cache.shape
    groups = queries.shape[1] // (kv_local * head_dim)
    width = hidden_in.shape[1]
    query_heads = queries.reshape(rows_dev, kv_local, groups, head_dim)
    scores = jnp.einsum(
        "rhgd,rhld->rhgl", query_heads, key_cache, preferred_element_type=jnp.float32
    ) * (1.0 / math.sqrt(head_dim))
    valid_mask = (jnp.arange(cache_len, dtype=jnp.int32)[None, :] < cache_lengths[:, None])[
        :, None, None, :
    ]
    scores = jnp.where(valid_mask, scores, -jnp.inf)
    largest = jnp.max(scores, axis=-1, keepdims=True)
    exponent = jnp.exp(scores - largest)
    attn_probs = (exponent / jnp.sum(exponent, axis=-1, keepdims=True)).astype(jnp.bfloat16)
    attn_out = jnp.einsum(
        "rhgl,rhld->rhgd", attn_probs, cached_value_rows, preferred_element_type=jnp.float32
    ).astype(jnp.bfloat16)
    attn_out = attn_out.reshape(rows_dev, kv_local * groups * head_dim)

    E, _, ff = w_gate.shape
    R = max(8, E * CAP)
    share = width // T
    hl = attn_out.shape[1]
    cb = out_weight.shape[1]
    per = G // T
    bf16 = jnp.bfloat16
    f32 = jnp.float32
    vmem = pl.BlockSpec(memory_space=pltpu.VMEM)
    hbm = pl.BlockSpec(memory_space=pl.ANY)
    dma = pltpu.SemaphoreType.DMA
    return pl.pallas_call(
        functools.partial(layer_kernel, G, T, E, R),
        out_shape=jax.ShapeDtypeStruct((rows_dev, share), bf16),
        in_specs=[vmem] * 4 + [hbm] * 4,
        out_specs=vmem,
        scratch_shapes=[
            pltpu.VMEM((hl, cb), bf16),
            pltpu.VMEM((E, width, ff), bf16),
            pltpu.VMEM((E, width, ff), bf16),
            pltpu.VMEM((2, E, ff, SUB), bf16),
            pltpu.VMEM((G, rows_dev, hl), bf16),
            pltpu.VMEM((G, rows_dev, cb), bf16),
            pltpu.VMEM((T, per, rows_dev, cb), bf16),
            pltpu.VMEM((per, rows_dev, cb), bf16),
            pltpu.VMEM((G, rows_dev, cb), bf16),
            pltpu.VMEM((rows_dev, width), bf16),
            pltpu.VMEM((rows_dev, width), bf16),
            pltpu.VMEM((T, G, R, share), bf16),
            pltpu.VMEM((T, G, R, share), bf16),
            pltpu.VMEM((E, G * R, ff), f32),
            pltpu.VMEM((E, G * R, ff), f32),
            pltpu.VMEM((E, G * R, ff), bf16),
            pltpu.VMEM((T, G, R, share), bf16),
            pltpu.VMEM((G, T, R, share), bf16),
            pltpu.VMEM((rows_dev, G * R), bf16),
            pltpu.VMEM((rows_dev, G * T * R), f32),
            dma(()),
            dma((T,)),
            dma((T,)),
            dma((T * (share // SUB),)),
            dma((G,)),
            dma((G,)),
            dma((G,)),
            dma((G,)),
            dma((T, per)),
            dma((per, T)),
            dma((G,)),
            dma((T, G)),
            dma((T, G)),
            dma((T, G)),
            dma((G, T)),
        ],
        compiler_params=pltpu.CompilerParams(
            collective_id=0, has_side_effects=True, vmem_limit_bytes=66 * 1000 * 1000
        ),
    )(attn_out, hidden_in, expert_ids, route_probs, out_weight, w_gate, w_up, w_down)


def solution(mesh):
    placed = (
        P("dp", None),
        P("dp", "tensor"),
        P("dp", "tensor", None, None),
        P("dp", "tensor", None, None),
        P("dp"),
        P("tensor", "dp"),
        P("dp", None),
        P("dp", None),
        P(("dp", "tensor"), None, None),
        P(("dp", "tensor"), None, None),
        P(("dp", "tensor"), None, None),
    )
    return jax.shard_map(
        local, mesh=mesh, in_specs=placed, out_specs=P("dp", "tensor"), check_vma=False
    )
```

```python
import functools
import math

import jax
import jax.numpy as jnp
from jax import lax
from jax.experimental import pallas as pl
from jax.experimental.pallas import tpu as pltpu
from jax.sharding import PartitionSpec as P

CAP = 2
SUB = 512
INNER = 2
MESH = pl.DeviceIdType.MESH


def layer_kernel(
    G,
    T,
    E,
    R,
    attn_ref,
    hidden_ref,
    ids_ref,
    probs_ref,
    wo_hbm,
    wg_hbm,
    wu_hbm,
    wd_hbm,
    out_ref,
    wo,
    wg,
    wu,
    wd,
    gathered,
    partial,
    rs_recv,
    summed,
    proj,
    residual,
    normed,
    outgoing,
    arrived,
    acc_g,
    acc_u,
    act,
    outs,
    results,
    pick,
    table,
    wo_sem,
    wg_sem,
    wu_sem,
    wd_sem,
    s1,
    r1,
    sf,
    s2,
    r2,
    s3,
    r3,
    s4,
    r4,
    s5,
    r5,
):
    d = lax.axis_index("dp")
    t = lax.axis_index("tensor")
    rows, width = hidden_ref.shape
    share = width // T
    cb = wo.shape[1]
    per = G // T
    ff = wg.shape[2]
    subs = share // SUB
    f32 = jnp.float32
    bf16 = jnp.bfloat16

    def remote(src, dst, ss, rs, dd, tt):
        return pltpu.make_async_remote_copy(
            src_ref=src,
            dst_ref=dst,
            send_sem=ss,
            recv_sem=rs,
            device_id=(dd, tt),
            device_id_type=MESH,
        )

    barrier = pltpu.get_barrier_semaphore()

    def greet(i, c):
        o = lax.rem(d * T + t + i, G * T)
        pl.semaphore_signal(barrier, inc=1, device_id=(o // T, lax.rem(o, T)), device_id_type=MESH)
        return c

    lax.fori_loop(1, G * T, greet, 0)

    wo_copy = pltpu.make_async_copy(wo_hbm, wo, wo_sem)
    wo_copy.start()

    def part(j):
        return pl.ds(j * share, share)

    def g_copy(j):
        return pltpu.make_async_copy(wg_hbm.at[:, part(j), :], wg.at[:, part(j), :], wg_sem.at[j])

    def u_copy(j):
        return pltpu.make_async_copy(wu_hbm.at[:, part(j), :], wu.at[:, part(j), :], wu_sem.at[j])

    def d_copy(s):
        j = lax.rem(t + 1 + s // subs, T)
        col = pl.multiple_of(j * share + (s % subs) * SUB, SUB)
        return pltpu.make_async_copy(wd_hbm.at[:, :, pl.ds(col, SUB)], down_at(s), wd_sem.at[s])

    def down_at(s):
        if s < 2:
            return wd.at[s]
        k = (s - 2) // 2
        return (wg, wu)[s % 2].at[:, k * share : k * share + ff, 0:SUB]

    subs_all = T * subs

    pl.semaphore_wait(barrier, G * T - 1)

    outer = G // INNER
    inner = lax.rem(d, INNER)
    mate = d + 1 - 2 * inner

    def far(i):
        return lax.rem(d + INNER * i, G)

    def first(p):
        return remote(attn_ref, gathered.at[d], s1.at[p], r1.at[d], p, t)

    first(mate).start()

    def send1(i, c):
        first(far(i)).start()
        return c

    lax.fori_loop(1, outer, send1, 0)
    def fetch(j):
        g_copy(j).start()
        u_copy(j).start()

    fetch(0)
    gathered[d] = attn_ref[...]

    ids = ids_ref[...].T
    probs = probs_ref[...].T
    shares = probs / jnp.sum(probs, axis=-1, keepdims=True)
    below = lax.broadcasted_iota(jnp.int32, (rows, rows), 0) > lax.broadcasted_iota(
        jnp.int32, (rows, rows), 1
    )
    below = jnp.where(below, 1.0, 0.0).astype(bf16)

    def routes(count, device_of):
        col = lax.broadcasted_iota(jnp.int32, (rows, count), 1)
        place = lax.rem(col, R)
        expert = device_of(lax.div(col, R)) * E + lax.div(place, CAP)
        slot = lax.rem(place, CAP)
        assigned = jnp.zeros((rows, count), f32)
        weight = jnp.zeros((rows, count), f32)
        for k in range(ids.shape[1]):
            same = ids[:, k : k + 1] == expert
            assigned = assigned + jnp.where(same, 1.0, 0.0)
            weight = weight + jnp.where(same, shares[:, k : k + 1], 0.0)
        rank = jnp.dot(below, assigned.astype(bf16), preferred_element_type=f32)
        hit = (assigned > 0.5) & (rank.astype(jnp.int32) == slot) & (place < E * CAP)
        return hit, weight

    hit, weight = routes(G * T * R, lambda n: n)
    table[...] = jnp.where(hit, weight, 0.0)
    hit, weight = routes(G * R, lambda n: n * T + t)
    pick[...] = jnp.where(hit, 1.0, 0.0).astype(bf16)
    wo_copy.wait()

    def project(i, c):
        near = i < outer + 1
        k = jnp.where(near, i - 1, i - outer)
        base = lax.rem(d + G - INNER * k, G)
        straight = jnp.logical_and(i > 1, near)
        g = jnp.where(i == 0, d, jnp.where(straight, base, base + 1 - 2 * inner))

        @pl.when(i > 0)
        def _():
            remote(attn_ref, gathered.at[g], s1.at[g], r1.at[g], g, t).wait_recv()

        @pl.when(straight)
        def _():
            remote(gathered.at[g], gathered.at[g], sf.at[g], r1.at[g], mate, t).start()

        @pl.when(i == outer)
        def _():
            fetch(1)

        partial[g] = jnp.dot(gathered[g], wo[...], preferred_element_type=f32).astype(bf16)
        owner = g // per

        @pl.when(owner != t)
        def _():
            remote(
                partial.at[g], rs_recv.at[t, lax.rem(g, per)], s2.at[g], r2.at[t, lax.rem(g, per)], d, owner
            ).start()

        return c

    lax.fori_loop(0, G, project, 0)
    for j in range(2, T - 1):
        fetch(j)

    def reduce(k, c):
        g = t * per + k
        total = partial[g].astype(f32)
        for o in range(1, T):
            src = lax.rem(t + o, T)
            remote(partial.at[g], rs_recv.at[src, k], s2.at[g], r2.at[src, k], d, src).wait_recv()
            total = total + rs_recv[src, k].astype(f32)
        summed[k] = total.astype(bf16)
        for tt in range(T):
            own = jnp.logical_and(g == d, t == tt)

            @pl.when(own)
            def _():
                proj[d] = summed[k]

            @pl.when(jnp.logical_not(own))
            def _():
                remote(summed.at[k], proj.at[d], s3.at[k, tt], r3.at[d], g, tt).start()

        return c

    lax.fori_loop(0, per, reduce, 0)

    fetch(T - 1)
    home = d // per

    def wait3(i, c):
        @pl.when(jnp.logical_not(jnp.logical_and(i == d, home == t)))
        def _():
            remote(summed.at[0], proj.at[i], s3.at[0, 0], r3.at[i], i, home).wait_recv()

        return c

    lax.fori_loop(0, G, wait3, 0)

    d_copy(0).start()
    d_copy(1).start()

    squares = jnp.zeros((rows, cb), f32)
    for g in range(G):
        cols = slice(g * cb, (g + 1) * cb)
        block = (hidden_ref[:, cols].astype(f32) + proj[g].astype(f32)).astype(bf16)
        residual[:, cols] = block
        bf = block.astype(f32)
        squares = squares + bf * bf
    scale = lax.rsqrt(jnp.sum(squares, axis=-1, keepdims=True) / width + 1e-06)
    for g in range(G):
        cols = slice(g * cb, (g + 1) * cb)
        normed[:, cols] = (residual[:, cols].astype(f32) * scale).astype(bf16)

    for j in range(T):
        block = lax.dot_general(
            pick[...],
            normed[:, j * share : (j + 1) * share],
            (((0,), (0,)), ((), ())),
            preferred_element_type=f32,
        )
        outgoing[j] = block.reshape(G, R, share).astype(bf16)
        arrived[j, d] = outgoing[j, d]

        def send4(i, c, j=j):
            p = lax.rem(d + i, G)
            remote(outgoing.at[j, p], arrived.at[j, d], s4.at[j, p], r4.at[j, d], p, t).start()
            return c

        lax.fori_loop(1, G, send4, 0)

    for j in range(T):

        def wait4(i, c, j=j):
            p = lax.rem(d + G - i, G)
            remote(outgoing.at[j, p], arrived.at[j, p], s4.at[j, p], r4.at[j, p], p, t).wait_recv()
            return c

        lax.fori_loop(1, G, wait4, 0)
        g_copy(j).wait()
        u_copy(j).wait()

        def up(e, c, j=j):
            x = arrived[j].astype(f32).reshape(G * R, share).astype(bf16)
            gp = jnp.dot(x, wg[e, j * share : (j + 1) * share, :], preferred_element_type=f32)
            uq = jnp.dot(x, wu[e, j * share : (j + 1) * share, :], preferred_element_type=f32)
            if j == 0:
                acc_g[e] = gp
                acc_u[e] = uq
            else:
                gp = acc_g[e] + gp
                uq = acc_u[e] + uq
                if j < T - 1:
                    acc_g[e] = gp
                    acc_u[e] = uq
                else:
                    slot = lax.rem(lax.broadcasted_iota(jnp.int32, (G * R, ff), 0), R)
                    mine = (slot // CAP) == e
                    value = gp / (1.0 + jnp.exp(-gp)) * uq
                    act[e] = jnp.where(mine, value, 0.0).astype(bf16)
            return c

        lax.fori_loop(0, E, up, 0)
        for s in (2 * j + 2, 2 * j + 3):
            if s < subs_all:
                d_copy(s).start()

    for s in range(T * subs):
        d_copy(s).wait()
        half = s % subs
        down = down_at(s)
        total = jnp.dot(act[0], down[0], preferred_element_type=f32)
        for e in range(1, E):
            total = total + jnp.dot(act[e], down[e], preferred_element_type=f32)
        n = s // subs
        outs[n, :, :, half * SUB : (half + 1) * SUB] = total.reshape(G, R, SUB).astype(bf16)
        if half == subs - 1:
            j = lax.rem(t + 1 + n, T)

            def send5(i, c, n=n, j=j):
                p = lax.rem(d + i, G)
                own = jnp.logical_and(p == d, j == t)

                @pl.when(own)
                def _():
                    results[d, t] = outs[n, p]

                @pl.when(jnp.logical_not(own))
                def _():
                    remote(
                        outs.at[n, p], results.at[d, t], s5.at[n, p], r5.at[d, t], p, j
                    ).start()

                return c

            lax.fori_loop(0, G, send5, 0)

    def wait5(i, c):
        o = lax.rem(d * T + t + i, G * T)
        p, q = o // T, lax.rem(o, T)
        remote(outs.at[0, p], results.at[p, q], s5.at[0, p], r5.at[p, q], p, q).wait_recv()
        return c

    lax.fori_loop(1, G * T, wait5, 0)
    back = results[...].astype(f32).reshape(G * T * R, share)
    mixture = jnp.dot(
        table[...], back, precision=lax.Precision.HIGHEST, preferred_element_type=f32
    )
    mine = residual[:, pl.ds(pl.multiple_of(t * share, share), share)].astype(f32)
    out_ref[...] = (mine + mixture).astype(bf16)

    def drain1(i, c):
        p = lax.rem(d + i, G)
        for j in range(T):
            remote(outgoing.at[j, p], arrived.at[j, d], s4.at[j, p], r4.at[j, d], p, t).wait_send()
        return c

    lax.fori_loop(1, G, drain1, 0)
    first(mate).wait_send()

    def drain0(i, c):
        first(far(i)).wait_send()
        g = far(i)
        remote(gathered.at[g], gathered.at[g], sf.at[g], r1.at[g], mate, t).wait_send()
        return c

    lax.fori_loop(1, outer, drain0, 0)

    def drain2(g, c):
        owner = g // per

        @pl.when(owner != t)
        def _():
            remote(partial.at[g], rs_recv.at[t, 0], s2.at[g], r2.at[t, 0], d, owner).wait_send()

        for n in range(T):
            j = lax.rem(t + 1 + n, T)

            @pl.when(jnp.logical_not(jnp.logical_and(g == d, j == t)))
            def _():
                remote(outs.at[n, g], results.at[d, t], s5.at[n, g], r5.at[d, t], g, j).wait_send()

        return c

    lax.fori_loop(0, G, drain2, 0)

    def drain3(k, c):
        g = t * per + k
        for tt in range(T):

            @pl.when(jnp.logical_not(jnp.logical_and(g == d, t == tt)))
            def _():
                remote(summed.at[k], proj.at[d], s3.at[k, tt], r3.at[d], g, tt).wait_send()

        return c

    lax.fori_loop(0, per, drain3, 0)


def local(
    hidden_in,
    queries,
    key_cache,
    cached_value_rows,
    cache_lengths,
    out_weight,
    expert_ids,
    route_probs,
    w_gate,
    w_up,
    w_down,
):
    G = lax.axis_size("dp")
    T = lax.axis_size("tensor")
    tp_rank = lax.axis_index("tensor")
    rows_dev, kv_local, cache_len, head_dim = key_cache.shape
    groups = queries.shape[1] // (kv_local * head_dim)
    width = hidden_in.shape[1]
    query_heads = queries.reshape(rows_dev, kv_local, groups, head_dim)
    scores = jnp.einsum(
        "rhgd,rhld->rhgl", query_heads, key_cache, preferred_element_type=jnp.float32
    ) * (1.0 / math.sqrt(head_dim))
    valid_mask = (jnp.arange(cache_len, dtype=jnp.int32)[None, :] < cache_lengths[:, None])[
        :, None, None, :
    ]
    scores = jnp.where(valid_mask, scores, -jnp.inf)
    largest = jnp.max(scores, axis=-1, keepdims=True)
    exponent = jnp.exp(scores - largest)
    attn_probs = (exponent / jnp.sum(exponent, axis=-1, keepdims=True)).astype(jnp.bfloat16)
    attn_out = jnp.einsum(
        "rhgl,rhld->rhgd", attn_probs, cached_value_rows, preferred_element_type=jnp.float32
    ).astype(jnp.bfloat16)
    attn_out = attn_out.reshape(rows_dev, kv_local * groups * head_dim)

    E, _, ff = w_gate.shape
    R = max(8, E * CAP)
    share = width // T
    hl = attn_out.shape[1]
    cb = out_weight.shape[1]
    per = G // T
    bf16 = jnp.bfloat16
    f32 = jnp.float32
    vmem = pl.BlockSpec(memory_space=pltpu.VMEM)
    hbm = pl.BlockSpec(memory_space=pl.ANY)
    dma = pltpu.SemaphoreType.DMA
    return pl.pallas_call(
        functools.partial(layer_kernel, G, T, E, R),
        out_shape=jax.ShapeDtypeStruct((rows_dev, share), bf16),
        in_specs=[vmem] * 4 + [hbm] * 4,
        out_specs=vmem,
        scratch_shapes=[
            pltpu.VMEM((hl, cb), bf16),
            pltpu.VMEM((E, width, ff), bf16),
            pltpu.VMEM((E, width, ff), bf16),
            pltpu.VMEM((2, E, ff, SUB), bf16),
            pltpu.VMEM((G, rows_dev, hl), bf16),
            pltpu.VMEM((G, rows_dev, cb), bf16),
            pltpu.VMEM((T, per, rows_dev, cb), bf16),
            pltpu.VMEM((per, rows_dev, cb), bf16),
            pltpu.VMEM((G, rows_dev, cb), bf16),
            pltpu.VMEM((rows_dev, width), bf16),
            pltpu.VMEM((rows_dev, width), bf16),
            pltpu.VMEM((T, G, R, share), bf16),
            pltpu.VMEM((T, G, R, share), bf16),
            pltpu.VMEM((E, G * R, ff), f32),
            pltpu.VMEM((E, G * R, ff), f32),
            pltpu.VMEM((E, G * R, ff), bf16),
            pltpu.VMEM((T, G, R, share), bf16),
            pltpu.VMEM((G, T, R, share), bf16),
            pltpu.VMEM((rows_dev, G * R), bf16),
            pltpu.VMEM((rows_dev, G * T * R), f32),
            dma(()),
            dma((T,)),
            dma((T,)),
            dma((T * (share // SUB),)),
            dma((G,)),
            dma((G,)),
            dma((G,)),
            dma((G,)),
            dma((T, per)),
            dma((per, T)),
            dma((G,)),
            dma((T, G)),
            dma((T, G)),
            dma((T, G)),
            dma((G, T)),
        ],
        compiler_params=pltpu.CompilerParams(
            collective_id=0, has_side_effects=True, vmem_limit_bytes=66 * 1000 * 1000
        ),
    )(attn_out, hidden_in, expert_ids.T, route_probs.T, out_weight, w_gate, w_up, w_down)


def solution(mesh):
    placed = (
        P("dp", None),
        P("dp", "tensor"),
        P("dp", "tensor", None, None),
        P("dp", "tensor", None, None),
        P("dp"),
        P("tensor", "dp"),
        P("dp", None),
        P("dp", None),
        P(("dp", "tensor"), None, None),
        P(("dp", "tensor"), None, None),
        P(("dp", "tensor"), None, None),
    )
    return jax.shard_map(
        local, mesh=mesh, in_specs=placed, out_specs=P("dp", "tensor"), check_vma=False
    )
```
